32 devices in a mesh: ctx: 16 (over z, x, core), tp: 2 (over y).
Axes of the slice: x: 2, y: 2, z: 4, core: 2. Of those that a mesh axis runs over, the one named last changes fastest.
Arguments:
- token_ids: int32 [2048], P('ctx'), may hold values from 0 to 511
- stream_table: bfloat16 [3, 512, 4096], P(None, None, 'tp'), may hold values from -6 to 6
- filters: float32 [256, 128], P('tp'), may hold values from -4 to 4
- proj_qk: bfloat16 [4096, 2, 4096], P(None, None, 'tp'), may hold values from -4 to 4
Outputs:
- attended: bfloat16 [2048, 4096], P('ctx', 'tp')
The draws below stay inside these ranges and needn't reach their ends.
All inputs are finite; a program needn't handle non-finite values.
Results may differ from the reference program's by a relative error of at most 0.01.
Values may be sent and summed in bfloat16 or wider, within the bound.
A program may use at most 128 MiB of HBM per device.

```python
import math
import jax
import jax.numpy as jnp
import numpy as np
from jax import lax

VOCAB = 512
CH = 4096
HEADS = 32
HEAD = 128
GROUP = 16
FLEN = 128
SPAN = 8
TOK_DEV = 128
TOKENS = 2048
GROUPS = 256


def draw_filters(key, part):
    tau_key, tap_key = jax.random.split(key)
    tau = jnp.exp(jax.random.uniform(tau_key, (GROUPS, 1), jnp.float32, math.log(8.0), math.log(4000.0)))
    lag_value = jnp.arange(FLEN, dtype=jnp.float32)[None, :]
    envelope = jnp.exp(-lag_value / tau)
    normal_size = jnp.sqrt((1.0 - jnp.exp(-2.0 * FLEN / tau)) / (1.0 - jnp.exp(-2.0 / tau)))
    taps = jax.random.truncated_normal(tap_key, -4.0, 4.0, (GROUPS, FLEN), jnp.float32)
    return taps * envelope / normal_size


def draw_proj_qk(key, part):
    query_key, key_key = jax.random.split(key, 2)
    scale = CH ** (-0.5)
    query_part = jax.random.truncated_normal(query_key, -4.0, 4.0, (CH, CH), jnp.float32) * scale
    key_part = jax.random.truncated_normal(key_key, -4.0, 4.0, (CH, CH), jnp.float32) * scale
    return jnp.stack([query_part, key_part], axis=1).astype(jnp.bfloat16)


def touch_ends(array, own_key, least, largest):
    index_at = [jax.random.randint(jax.random.fold_in(own_key, axis), (), 0, length) for axis, length in enumerate(array.shape)]
    longest = array.shape.index(max(array.shape))
    neighbour = index_at[:longest] + [(index_at[longest] + 1) % array.shape[longest]] + index_at[longest + 1:]
    return array.at[tuple(index_at)].set(least).at[tuple(neighbour)].set(largest)


def block_scale(rng, dims, cuts, low, high):
    def one(axis_at, blocks):
        steps = jax.random.uniform(jax.random.fold_in(jax.random.fold_in(rng, 6), axis_at), (blocks,), jnp.float32, low / len(cuts), high / len(cuts))
        return jnp.repeat(jnp.exp(steps), dims[axis_at] // blocks).reshape((-1,) + (1,) * (len(dims) - axis_at - 1))

    gain = one(*cuts[0])
    for cut in cuts[1:]:
        gain = gain * one(*cut)
    return gain


def cumulative_ranks(count, lean):
    loads = [(1 << 20) // math.isqrt(standing ** lean) + 1 for standing in range(1, count + 1)]
    spread = 1 + sum(loads) // (1 << 30)
    return np.cumsum(np.array([max(1, weight // spread) for weight in loads]))


def ranked_ids(key, shape, count, skew):
    grid = cumulative_ranks(count, skew)
    lot = jax.random.randint(jax.random.fold_in(key, 1), shape, 0, int(grid[count - 1]))
    standing = jnp.searchsorted(jnp.asarray(grid, jnp.int32), lot, side="right")
    return jax.random.permutation(jax.random.fold_in(key, 2), count)[standing].astype(jnp.int32)


def centred(key, shape, scale, most, pieces=(), held_as=jnp.bfloat16):
    entries = jax.random.normal(key, shape, jnp.float32) * scale
    if len(pieces) > 0:
        entries = block_scale(key, shape, pieces, -0.22, 0.18) * entries
    return jnp.clip(entries, min=-most, max=most).astype(held_as)


def setup_inputs(seed: int = 0) -> dict:
    key_list = jax.random.split(jax.random.key(seed), 5)
    token_ids = touch_ends(ranked_ids(key_list[0], (TOKENS,), VOCAB, 2), jax.random.fold_in(key_list[0], 3), 0, VOCAB - 1).astype(jnp.int32)
    stream_table = centred(key_list[1], (3, VOCAB, CH), 1.0, 6.0, ((2, 2),))
    filters = draw_filters(jax.random.fold_in(key_list[4], 71), 0)
    proj_qk = draw_proj_qk(jax.random.fold_in(key_list[4], 71), 0)
    return dict(token_ids=token_ids, stream_table=stream_table, filters=filters, proj_qk=proj_qk)


def head_attention(query_block, key_block, value_block, allowed):
    scores = jnp.dot(query_block, key_block.T, preferred_element_type=jnp.float32) * (HEAD ** -0.5)
    scores = jnp.where(allowed, scores, -jnp.inf)
    row_max = jnp.max(scores, axis=1, keepdims=True)
    weights = jnp.where(allowed, jnp.exp(scores - row_max), 0.0)
    row_sum = jnp.sum(weights, axis=1, keepdims=True)
    mixed = jnp.dot(weights.astype(jnp.bfloat16), value_block, preferred_element_type=jnp.float32)
    return mixed / row_sum


def reference(token_ids, stream_table, filters, proj_qk):
    streams = jnp.take(stream_table, token_ids, axis=1)
    post_gate = streams[0].astype(jnp.float32)
    mixed_in = (streams[1].astype(jnp.float32) * streams[2].astype(jnp.float32)).astype(jnp.bfloat16)
    taps = jnp.repeat(filters, GROUP, axis=0)
    padded = jnp.concatenate([jnp.zeros((FLEN - 1, CH), jnp.float32), mixed_in.astype(jnp.float32)], axis=0)

    def add_lag(lag_index, running):
        window = lax.dynamic_slice_in_dim(padded, FLEN - 1 - lag_index, TOKENS, 0)
        column = lax.dynamic_slice_in_dim(taps, lag_index, 1, 1)
        return running + window * column[:, 0][None, :]

    conv = lax.fori_loop(0, FLEN, add_lag, jnp.zeros((TOKENS, CH), jnp.float32))
    gated = (post_gate * conv).astype(jnp.bfloat16)
    queries = jnp.dot(gated, proj_qk[:, 0, :], preferred_element_type=jnp.float32).astype(jnp.bfloat16)
    keys = jnp.dot(gated, proj_qk[:, 1, :], preferred_element_type=jnp.float32).astype(jnp.bfloat16)
    reach = (SPAN - 1) * TOK_DEV
    key_pad = jnp.concatenate([jnp.zeros((reach, CH), jnp.bfloat16), keys], axis=0)
    value_pad = jnp.concatenate([jnp.zeros((reach, CH), jnp.bfloat16), gated], axis=0)

    def one_block(block_index):
        first = (block_index * TOK_DEV).astype(jnp.int32)
        query_block = lax.dynamic_slice_in_dim(queries, first, TOK_DEV, 0).reshape(TOK_DEV, HEADS, HEAD)
        key_block = lax.dynamic_slice_in_dim(key_pad, first, SPAN * TOK_DEV, 0).reshape(SPAN * TOK_DEV, HEADS, HEAD)
        value_block = lax.dynamic_slice_in_dim(value_pad, first, SPAN * TOK_DEV, 0).reshape(SPAN * TOK_DEV, HEADS, HEAD)
        query_pos = first + jnp.arange(TOK_DEV, dtype=jnp.int32)
        key_pos = first - reach + jnp.arange(SPAN * TOK_DEV, dtype=jnp.int32)
        allowed = (key_pos[None, :] >= 0) & (key_pos[None, :] <= query_pos[:, None])

        def one_head(trio):
            return head_attention(trio[0], trio[1], trio[2], allowed)

        per_head = lax.map(one_head, (jnp.transpose(query_block, (1, 0, 2)), jnp.transpose(key_block, (1, 0, 2)), jnp.transpose(value_block, (1, 0, 2))))
        return jnp.transpose(per_head, (1, 0, 2)).reshape(TOK_DEV, CH)

    blocks_out = lax.map(one_block, jnp.arange(TOKENS // TOK_DEV, dtype=jnp.int32))
    return blocks_out.reshape(TOKENS, CH).astype(jnp.bfloat16)
```

```python
import functools
import jax
import jax.numpy as jnp
from jax import lax
from jax.experimental import pallas as pl
from jax.experimental.pallas import tpu as pltpu
from jax.sharding import PartitionSpec as P

HEAD = 128
GROUP = 16
FLEN = 128
SPAN = 8
LANE = 128
PLANE = 4
BACK = SPAN - 1
SLOTS = BACK + PLANE
MESH = pl.DeviceIdType.MESH
F32, BF16 = jnp.float32, jnp.bfloat16


def lanes(index, width=LANE):
    return pl.ds(pl.multiple_of(index * width, LANE), width)


def rows(index, count=1):
    return pl.ds(pl.multiple_of(index * FLEN, FLEN), count * FLEN)


def dot(a, b):
    return jnp.dot(a, b, preferred_element_type=F32)


def wait_ahead(barrier, ahead, always, each):
    for planes in range(3):
        @pl.when(ahead == planes if planes < 2 else ahead >= planes)
        def _():
            pl.semaphore_wait(barrier, always + planes * each)


def ids_kernel(count, ids_ref, out_ref, buf, send, recv):
    me = lax.axis_index("ctx")
    plane, place = me // PLANE, me % PLANE
    planes = count // PLANE
    buf[...] = jnp.full(buf.shape, -1, jnp.int32)
    buf[2 * PLANE + place] = ids_ref[...]
    barrier = pltpu.get_barrier_semaphore()

    def partners(sign, act):
        for dist in range(3):
            for other in range(PLANE):
                there = plane + sign * dist
                ok = (there >= 0) & (there < planes)
                if dist == 0:
                    ok = ok & (other != place)
                pl.when(ok)(functools.partial(act, dist, other, there * PLANE + other))

    def greet(dist, other, device):
        pl.semaphore_signal(barrier, inc=1, device_id={"ctx": device}, device_id_type=MESH)

    def copy_to(dist, other, device):
        return pltpu.make_async_remote_copy(
            src_ref=ids_ref,
            dst_ref=buf.at[2 * PLANE + place - dist * PLANE],
            send_sem=send.at[dist * PLANE + other],
            recv_sem=recv.at[2 * PLANE + place - dist * PLANE],
            device_id={"ctx": device},
            device_id_type=MESH,
        )

    def arrived(dist, other, device):
        slot = 2 * PLANE + other - dist * PLANE
        pltpu.make_async_remote_copy(
            src_ref=ids_ref, dst_ref=buf.at[slot], send_sem=send.at[0], recv_sem=recv.at[slot],
            device_id={"ctx": device}, device_id_type=MESH,
        ).wait_recv()

    partners(-1, greet)
    wait_ahead(barrier, planes - 1 - plane, PLANE - 1, PLANE)
    partners(1, lambda *a: copy_to(*a).start())
    partners(-1, arrived)
    partners(1, lambda *a: copy_to(*a).wait_send())
    out_ref[...] = buf[...]


def share_ids(token_ids, count):
    return pl.pallas_call(
        functools.partial(ids_kernel, count),
        out_shape=jax.ShapeDtypeStruct((3 * PLANE, 1, FLEN), jnp.int32),
        in_specs=[pl.BlockSpec(memory_space=pltpu.VMEM)],
        out_specs=pl.BlockSpec(memory_space=pltpu.VMEM),
        scratch_shapes=[
            pltpu.VMEM((3 * PLANE, 1, FLEN), jnp.int32),
            pltpu.SemaphoreType.DMA((3 * PLANE,)),
            pltpu.SemaphoreType.DMA((3 * PLANE,)),
        ],
        compiler_params=pltpu.CompilerParams(collective_id=0, has_side_effects=True),
        name="share_ids",
    )(token_ids.reshape(1, FLEN))


def conv_kernel(ids_ref, table_ref, taps_ref, gated_ref, value_ref, onehot, toep, mixed, post):
    width = gated_ref.shape[1]
    part = value_ref.shape[1]
    vocab = table_ref.shape[1]
    place = lax.axis_index("ctx") % PLANE

    def mark(block, _):
        ids = jnp.transpose(jnp.broadcast_to(ids_ref[block].astype(F32), (FLEN, FLEN)))
        word = lax.broadcasted_iota(jnp.int32, (FLEN, LANE), 1).astype(F32)
        for at in range(vocab // LANE):
            onehot[rows(block), at * LANE:(at + 1) * LANE] = (ids == word + float(at * LANE)).astype(F32).astype(BF16)
        return 0

    lax.fori_loop(0, 3 * PLANE, mark, 0)
    tap = lax.broadcasted_iota(jnp.int32, (FLEN, 2 * FLEN), 0)
    spot = lax.broadcasted_iota(jnp.int32, (FLEN, 2 * FLEN), 1)
    flip = (spot + tap == FLEN).astype(F32).astype(BF16)
    per = LANE // GROUP

    def build(column):
        line = dot(taps_ref[pl.ds(pl.multiple_of(column * per, per), per), :].astype(BF16), flip)
        for g in range(per):
            spread = jnp.broadcast_to(line[g:g + 1], (FLEN, 2 * FLEN))
            toep[g * FLEN:(g + 1) * FLEN] = pltpu.roll(spread, 0, 1, stride=1, stride_axis=0).astype(BF16)

    group_of = lax.broadcasted_iota(jnp.int32, (FLEN, LANE), 1) // GROUP

    def convolve(window):
        every = dot(toep[...], window)
        total = every[:FLEN]
        for g in range(1, per):
            total = jnp.where(group_of == g, every[g * FLEN:(g + 1) * FLEN], total)
        return total

    def own(column, _):
        cols = lanes(column)
        pair = jnp.concatenate([table_ref[1, :, cols], table_ref[2, :, cols]], axis=1)
        both = dot(onehot[rows(BACK + place, 2), :], pair)
        window = (both[:, :LANE] * both[:, LANE:]).astype(BF16)
        gate = dot(onehot[rows(BACK + 1 + place), :], table_ref[0, :, cols])
        build(column)
        gated_ref[:, cols] = (gate * convolve(window)).astype(BF16)
        return 0

    lax.fori_loop(0, width // LANE, own, 0)

    def shared(step, _):
        column = place * (part // LANE) + step
        cols = lanes(column)
        pair = jnp.concatenate([table_ref[1, :, cols], table_ref[2, :, cols]], axis=1)
        build(column)

        def fill(block, _):
            marks = onehot[rows(block), :]
            both = dot(marks, pair)
            mixed[rows(block), :] = (both[:, :LANE] * both[:, LANE:]).astype(BF16)
            post[rows(block), :] = dot(marks, table_ref[0, :, cols])
            return 0

        lax.fori_loop(0, 3 * PLANE, fill, 0)

        def window_of(block, _):
            conv = convolve(mixed[rows(block, 2), :])
            value_ref[rows(block), lanes(step)] = (post[rows(block + 1), :] * conv).astype(BF16)
            return 0

        lax.fori_loop(0, SLOTS, window_of, 0)
        return 0

    lax.fori_loop(0, part // LANE, shared, 0)


def gated_and_values(ids, table, filters):
    width = table.shape[2]
    vmem = pl.BlockSpec(memory_space=pltpu.VMEM)
    return pl.pallas_call(
        conv_kernel,
        out_shape=(
            jax.ShapeDtypeStruct((FLEN, width), BF16),
            jax.ShapeDtypeStruct((SLOTS * FLEN, width // PLANE), BF16),
        ),
        in_specs=[vmem] * 3,
        out_specs=(vmem, vmem),
        scratch_shapes=[
            pltpu.VMEM((3 * PLANE * FLEN, table.shape[1]), BF16),
            pltpu.VMEM((LANE // GROUP * FLEN, 2 * FLEN), BF16),
            pltpu.VMEM((3 * PLANE * FLEN, LANE), BF16),
            pltpu.VMEM((3 * PLANE * FLEN, LANE), F32),
        ],
        compiler_params=pltpu.CompilerParams(vmem_limit_bytes=40 << 20),
        name="gated_and_values",
    )(ids, table, filters)


def attend_kernel(
    count, shares, gated_ref, value_ref, weight_ref, out_ref,
    gall, wide, held, acc, qsend, ksend, qbuf, kbuf, osend, obuf,
    gs, gr, ws, qs, qr, ks, kr, zs, os_, or_,
):
    width = gated_ref.shape[1]
    heads = width // HEAD
    part = width // PLANE
    heads_part = heads // PLANE
    me, mine = lax.axis_index("ctx"), lax.axis_index("tp")
    plane, place = me // PLANE, me % PLANE
    planes = count // PLANE

    def weights_copy(share, head):
        return pltpu.make_async_copy(
            weight_ref.at[pl.ds(share * width, width), head],
            held.at[head, pl.ds(share * width, width)],
            ws.at[share, head],
        )

    for step in range(shares):
        for head in range(heads):
            weights_copy((mine + step) % shares, head).start()

    kbuf[:BACK * FLEN] = jnp.zeros((BACK * FLEN, part), BF16)
    barrier = pltpu.get_barrier_semaphore()

    def greet(**device):
        pl.semaphore_signal(barrier, inc=1, device_id=device, device_id_type=MESH)

    for step in range(1, shares):
        greet(tp=(mine + step) % shares)
    for step in range(1, PLANE):
        greet(ctx=plane * PLANE + (place + step) % PLANE)
    for dist in (1, 2):
        @pl.when(plane >= dist)
        def _():
            greet(ctx=me - dist * PLANE)
    wait_ahead(barrier, planes - 1 - plane, shares - 1 + PLANE - 1, 1)

    def remote(src, dst, send, recv, **device):
        return pltpu.make_async_remote_copy(
            src_ref=src, dst_ref=dst, send_sem=send, recv_sem=recv, device_id=device, device_id_type=MESH
        )

    def gated_copy(step, slot):
        return remote(gated_ref, gall.at[slot], gs.at[step], gr.at[slot], tp=(mine + step) % shares)

    for step in range(1, shares):
        gated_copy(step, mine).start()
    gall[mine] = gated_ref[...]

    src = lax.broadcasted_iota(jnp.int32, (LANE, 4 * LANE), 0)
    dst = lax.broadcasted_iota(jnp.int32, (LANE, 4 * LANE), 1)
    spread = (dst == jnp.where(dst < 2 * LANE, 2 * src, 2 * src + 1 + 2 * LANE)).astype(F32).astype(BF16)
    paired = held.reshape(heads, 2 * shares * width, HEAD)
    depth = min(2 * width, 1024)

    def q_copy(group, slot):
        return remote(qsend.at[group], qbuf.at[slot], qs.at[group], qr.at[slot], ctx=plane * PLANE + group)

    def k_copy(group, slot):
        return remote(ksend.at[group], kbuf.at[rows(BACK + slot)], ks.at[group], kr.at[BACK + slot], ctx=plane * PLANE + group)

    def z_copy(dist, slot):
        to = BACK + slot - dist * PLANE
        return remote(kbuf.at[rows(BACK + slot)], kbuf.at[rows(to)], zs.at[dist - 1, slot], kr.at[to], ctx=me + dist * PLANE)

    def pass_on(slot, act):
        @pl.when(plane + 1 < planes)
        def _():
            act(z_copy(1, slot))

        @pl.when((plane + 2 < planes) & (slot >= 1))
        def _():
            act(z_copy(2, slot))

    def project(step, share, head):
        base = share * 2 * width

        def chunk(at, total):
            take = pl.ds(pl.multiple_of(base + at * depth, LANE), depth)
            block = jnp.concatenate([paired[head, take, :], paired[head + 1, take, :]], axis=1)
            return total + dot(wide[:, lanes(at, depth)], block)

        first = jnp.zeros((2 * FLEN, 2 * HEAD), F32) if step == 0 else acc[head // 2]
        return lax.fori_loop(0, 2 * width // depth, chunk, first)

    for step in range(shares):
        share = (mine + step) % shares
        if step > 0:
            gated_copy(step, share).wait_recv()

        def widen(column, _):
            both = dot(gall[share, :, lanes(column)], spread).astype(BF16)
            wide[:FLEN, lanes(column, 2 * LANE)] = both[:, :2 * LANE]
            wide[FLEN:, lanes(column, 2 * LANE)] = both[:, 2 * LANE:]
            return 0

        lax.fori_loop(0, width // LANE, widen, 0)
        for head in range(0, heads, 2):
            weights_copy(share, head).wait()
            weights_copy(share, head + 1).wait()
            total = project(step, share, head)
            if step < shares - 1:
                acc[head // 2] = total
                continue
            for one in range(2):
                group, at = (head + one) // heads_part, (head + one) % heads_part
                cut = total[:, one * HEAD:(one + 1) * HEAD].astype(BF16)
                qsend[group, :, at * HEAD:(at + 1) * HEAD] = cut[:FLEN]
                ksend[group, :, at * HEAD:(at + 1) * HEAD] = cut[FLEN:]
                if at == heads_part - 1:
                    @pl.when(group != place)
                    def _():
                        k_copy(group, place).start()
                        q_copy(group, place).start()

                    @pl.when(group == place)
                    def _():
                        kbuf[rows(BACK + place), :] = ksend[group]
                        qbuf[place] = qsend[group]
                        pass_on(place, lambda c: c.start())

    for step in range(1, PLANE):
        slot = (place + step) % PLANE
        k_copy(slot, slot).wait_recv()
        pass_on(slot, lambda c: c.start())
    for step in range(1, PLANE):
        slot = (place + step) % PLANE
        q_copy(slot, slot).wait_recv()
    for dist in (1, 2):
        @pl.when(plane >= dist)
        def _():
            for slot in range(dist - 1, PLANE):
                z_copy(dist, slot).wait_recv()

    def o_copy(group, slot):
        return remote(osend.at[group], obuf.at[slot], os_.at[group], or_.at[slot], ctx=plane * PLANE + group)

    key_at = lax.broadcasted_iota(jnp.int32, (FLEN, SPAN * FLEN), 1)
    query_at = lax.broadcasted_iota(jnp.int32, (FLEN, SPAN * FLEN), 0)
    for block in range(PLANE):
        least = (BACK - block - plane * PLANE) * FLEN
        allowed = (key_at <= query_at + BACK * FLEN) & (key_at >= least)

        def one_head(head, _):
            keys = kbuf[block * FLEN:(block + SPAN) * FLEN, lanes(head)]
            values = value_ref[block * FLEN:(block + SPAN) * FLEN, lanes(head)]
            scores = lax.dot_general(
                qbuf[block, :, lanes(head)], keys, (((1,), (1,)), ((), ())), preferred_element_type=F32
            ) * HEAD ** (-0.5)
            scores = jnp.where(allowed, scores, -1e30)
            weights = jnp.exp(scores - jnp.max(scores, axis=1, keepdims=True))
            row_sum = jnp.sum(weights, axis=1, keepdims=True)
            osend[block, :, lanes(head)] = (dot(weights.astype(BF16), values) / row_sum).astype(BF16)
            return 0

        lax.fori_loop(0, heads_part, one_head, 0)

        @pl.when(block != place)
        def _():
            o_copy(block, place).start()

        @pl.when(block == place)
        def _():
            obuf[place] = osend[block]

    for step in range(1, PLANE):
        slot = (place + step) % PLANE
        o_copy(slot, slot).wait_recv()
    for slot in range(PLANE):
        out_ref[:, slot * part:(slot + 1) * part] = obuf[slot]
    for step in range(1, shares):
        gated_copy(step, mine).wait_send()
    for step in range(1, PLANE):
        slot = (place + step) % PLANE
        k_copy(slot, place).wait_send()
        q_copy(slot, place).wait_send()
        o_copy(slot, place).wait_send()
    for slot in range(PLANE):
        pass_on(slot, lambda c: c.wait_send())


def attended(gated, values, proj_qk, count, shares):
    width = gated.shape[1]
    heads, part = width // HEAD, width // PLANE
    channels = proj_qk.shape[0]
    by_head = proj_qk.reshape(channels, 2, heads, HEAD).transpose(0, 2, 1, 3)
    vmem = pl.BlockSpec(memory_space=pltpu.VMEM)
    dma = pltpu.SemaphoreType.DMA
    return pl.pallas_call(
        functools.partial(attend_kernel, count, shares),
        out_shape=jax.ShapeDtypeStruct((FLEN, width), BF16),
        in_specs=[vmem, vmem, pl.BlockSpec(memory_space=pl.ANY)],
        out_specs=vmem,
        scratch_shapes=[
            pltpu.VMEM((shares, FLEN, width), BF16),
            pltpu.VMEM((2 * FLEN, 2 * width), BF16),
            pltpu.VMEM((heads, channels, 2, HEAD), BF16),
            pltpu.VMEM((heads // 2, 2 * FLEN, 2 * HEAD), F32),
            pltpu.VMEM((PLANE, FLEN, part), BF16),
            pltpu.VMEM((PLANE, FLEN, part), BF16),
            pltpu.VMEM((PLANE, FLEN, part), BF16),
            pltpu.VMEM((SLOTS * FLEN, part), BF16),
            pltpu.VMEM((PLANE, FLEN, part), BF16),
            pltpu.VMEM((PLANE, FLEN, part), BF16),
            dma((shares,)), dma((shares,)), dma((shares, heads)),
            dma((PLANE,)), dma((PLANE,)), dma((PLANE,)), dma((SLOTS,)),
            dma((2, PLANE)), dma((PLANE,)), dma((PLANE,)),
        ],
        compiler_params=pltpu.CompilerParams(
            collective_id=1, has_side_effects=True, vmem_limit_bytes=60 << 20
        ),
        name="project_and_attend",
    )(gated, values, by_head)


def shards(token_ids, stream_table, filters, proj_qk):
    count, shares = lax.axis_size("ctx"), lax.axis_size("tp")
    ids = share_ids(token_ids, count)
    gated, values = gated_and_values(ids, stream_table, filters)
    return attended(gated, values, proj_qk, count, shares)


def solution(mesh):
    placed = (P("ctx"), P(None, None, "tp"), P("tp", None), P(None, None, "tp"))
    return jax.shard_map(
        shards, mesh=mesh, in_specs=placed, out_specs=P("ctx", "tp"), check_vma=False
    )
```

```python
import functools
import jax
import jax.numpy as jnp
from jax import lax
from jax.experimental import pallas as pl
from jax.experimental.pallas import tpu as pltpu
from jax.sharding import PartitionSpec as P

HEAD = 128
GROUP = 16
FLEN = 128
SPAN = 8
LANE = 128
PLANE = 4
BACK = SPAN - 1
SLOTS = BACK + PLANE
MESH = pl.DeviceIdType.MESH
F32, BF16 = jnp.float32, jnp.bfloat16


def lanes(index, width=LANE):
    return pl.ds(pl.multiple_of(index * width, LANE), width)


def rows(index, count=1):
    return pl.ds(pl.multiple_of(index * FLEN, FLEN), count * FLEN)


def dot(a, b):
    return jnp.dot(a, b, preferred_element_type=F32)


def wait_ahead(barrier, ahead, always, each):
    for planes in range(3):
        @pl.when(ahead == planes if planes < 2 else ahead >= planes)
        def _():
            pl.semaphore_wait(barrier, always + planes * each)


def whole_kernel(
    count, shares, ids_ref, taps_ref, table_ref, weight_ref, out_ref,
    idbuf, table, onehot, toep, mixed, post, values,
    gall, wide, held, acc, qsend, ksend, qbuf, kbuf, osend, obuf,
    ts, isend, irecv, gs, gr, ws, qs, qr, ks, kr, zs, os_, or_,
):
    width = out_ref.shape[1]
    heads = width // HEAD
    part = width // PLANE
    heads_part = heads // PLANE
    vocab = table.shape[1]
    me, mine = lax.axis_index("ctx"), lax.axis_index("tp")
    plane, place = me // PLANE, me % PLANE
    planes = count // PLANE

    def table_copy(stream):
        return pltpu.make_async_copy(table_ref.at[stream], table.at[stream], ts.at[stream])

    def weights_copy(share, head):
        return pltpu.make_async_copy(
            weight_ref.at[pl.ds(share * width, width), head],
            held.at[head, pl.ds(share * width, width)],
            ws.at[share, head],
        )

    for stream in range(3):
        table_copy(stream).start()
    for step in range(shares):
        for head in range(heads):
            weights_copy((mine + step) % shares, head).start()

    idbuf[...] = jnp.full(idbuf.shape, -1, jnp.int32)
    idbuf[2 * PLANE + place] = ids_ref[...]
    kbuf[:BACK * FLEN] = jnp.zeros((BACK * FLEN, part), BF16)
    barrier = pltpu.get_barrier_semaphore()

    def greet(**device):
        pl.semaphore_signal(barrier, inc=1, device_id=device, device_id_type=MESH)

    def partners(sign, act):
        for dist in range(3):
            for other in range(PLANE):
                there = plane + sign * dist
                ok = (there >= 0) & (there < planes)
                if dist == 0:
                    ok = ok & (other != place)
                pl.when(ok)(functools.partial(act, dist, other, there * PLANE + other))

    for step in range(1, shares):
        greet(tp=(mine + step) % shares)
    partners(-1, lambda dist, other, device: greet(ctx=device))
    ahead = planes - 1 - plane
    for some in range(3):
        @pl.when(ahead == some if some < 2 else ahead >= some)
        def _():
            pl.semaphore_wait(barrier, shares - 1 + PLANE - 1 + some * PLANE)

    def remote(src, dst, send, recv, **device):
        return pltpu.make_async_remote_copy(
            src_ref=src, dst_ref=dst, send_sem=send, recv_sem=recv, device_id=device, device_id_type=MESH
        )

    def ids_copy(dist, other, device):
        slot = 2 * PLANE + place - dist * PLANE
        return remote(ids_ref, idbuf.at[slot], isend.at[dist * PLANE + other], irecv.at[slot], ctx=device)

    def ids_here(dist, other, device):
        slot = 2 * PLANE + other - dist * PLANE
        remote(ids_ref, idbuf.at[slot], isend.at[0], irecv.at[slot], ctx=device).wait_recv()

    partners(1, lambda *a: ids_copy(*a).start())
    partners(-1, ids_here)

    def mark(block, _):
        ids = jnp.transpose(jnp.broadcast_to(idbuf[block].astype(F32), (FLEN, FLEN)))
        word = lax.broadcasted_iota(jnp.int32, (FLEN, LANE), 1).astype(F32)
        for at in range(vocab // LANE):
            onehot[rows(block), at * LANE:(at + 1) * LANE] = (ids == word + float(at * LANE)).astype(F32).astype(BF16)
        return 0

    lax.fori_loop(BACK + place, BACK + place + 2, mark, 0)
    row = lax.broadcasted_iota(jnp.int32, (FLEN, FLEN), 0)
    col = lax.broadcasted_iota(jnp.int32, (FLEN, FLEN), 1)
    flip = ((row + col == FLEN) | (row + col == 0)).astype(F32).astype(BF16)
    after = (row >= col).astype(F32).astype(BF16)
    before = (row < col).astype(F32).astype(BF16)
    per = LANE // GROUP

    def build(column):
        line = dot(taps_ref[pl.ds(pl.multiple_of(column * per, per), per), :].astype(BF16), flip)
        for g in range(per):
            turned = pltpu.roll(
                jnp.broadcast_to(line[g:g + 1], (FLEN, FLEN)), 0, 1, stride=1, stride_axis=0
            ).astype(BF16)
            toep[g * FLEN:(g + 1) * FLEN, :FLEN] = turned * before
            toep[g * FLEN:(g + 1) * FLEN, FLEN:] = turned * after

    def convolve(window):
        group_of = lax.broadcasted_iota(jnp.int32, (FLEN, window.shape[1]), 1) % LANE // GROUP
        total = dot(toep[:FLEN], window)
        for g in range(1, per):
            total = jnp.where(group_of == g, dot(toep[g * FLEN:(g + 1) * FLEN], window), total)
        return total

    def pair_of(cols):
        return jnp.concatenate([table[1, :, cols], table[2, :, cols]], axis=1)

    def own(column, _):
        cols = lanes(column)
        both = dot(onehot[rows(BACK + place, 2), :], pair_of(cols))
        window = (both[:, :LANE] * both[:, LANE:]).astype(BF16)
        gate = dot(onehot[rows(BACK + 1 + place), :], table[0, :, cols])
        build(column)
        gall[mine, :, cols] = (gate * convolve(window)).astype(BF16)
        return 0

    def gated_copy(step, slot, piece):
        cut = gall.at[slot, :, piece * part:(piece + 1) * part]
        return remote(cut, cut, gs.at[step, piece], gr.at[slot, piece], tp=(mine + step) % shares)

    for stream in range(3):
        table_copy(stream).wait()
    for piece in range(PLANE):
        lax.fori_loop(piece * (part // LANE), (piece + 1) * (part // LANE), own, 0)
        for step in range(1, shares):
            gated_copy(step, mine, piece).start()

    def shared(step):
        column = place * (part // LANE) + step
        cols = lanes(column)
        build(column)

        def fill(some, _):
            marks = onehot[pl.ds(pl.multiple_of(some * PLANE * FLEN, FLEN), PLANE * FLEN), :]
            here = pl.ds(pl.multiple_of(some * PLANE * FLEN, FLEN), PLANE * FLEN)
            both = dot(marks, pair_of(cols))
            mixed[here, :] = (both[:, :LANE] * both[:, LANE:]).astype(BF16)
            post[here, :] = dot(marks, table[0, :, cols])
            return 0

        lax.fori_loop(0, 3, fill, 0)

        def two_windows(twice, _):
            block = 2 * twice
            conv = convolve(jnp.concatenate([mixed[rows(block, 2), :], mixed[rows(block + 1, 2), :]], axis=1))
            values[rows(block), step * LANE:(step + 1) * LANE] = (post[rows(block + 1), :] * conv[:, :LANE]).astype(BF16)
            values[rows(block + 1), step * LANE:(step + 1) * LANE] = (post[rows(block + 2), :] * conv[:, LANE:]).astype(BF16)
            return 0

        lax.fori_loop(0, SLOTS // 2, two_windows, 0)
        conv = convolve(mixed[(SLOTS - 1) * FLEN:(SLOTS + 1) * FLEN, :])
        values[(SLOTS - 1) * FLEN:, step * LANE:(step + 1) * LANE] = (post[SLOTS * FLEN:, :] * conv).astype(BF16)

    src = lax.broadcasted_iota(jnp.int32, (LANE, 4 * LANE), 0)
    dst = lax.broadcasted_iota(jnp.int32, (LANE, 4 * LANE), 1)
    spread = (dst == jnp.where(dst < 2 * LANE, 2 * src, 2 * src + 1 + 2 * LANE)).astype(F32).astype(BF16)
    paired = held.reshape(heads, 2 * shares * width, HEAD)
    depth = min(2 * width, 1024)

    def q_copy(group, slot):
        return remote(qsend.at[group], qbuf.at[slot], qs.at[group], qr.at[slot], ctx=plane * PLANE + group)

    def k_copy(group, slot):
        return remote(ksend.at[group], kbuf.at[rows(BACK + slot)], ks.at[group], kr.at[BACK + slot], ctx=plane * PLANE + group)

    def z_copy(dist, slot):
        to = BACK + slot - dist * PLANE
        return remote(kbuf.at[rows(BACK + slot)], kbuf.at[rows(to)], zs.at[dist - 1, slot], kr.at[to], ctx=me + dist * PLANE)

    def pass_on(slot, act):
        @pl.when(plane + 1 < planes)
        def _():
            act(z_copy(1, slot))

        @pl.when((plane + 2 < planes) & (slot >= 1))
        def _():
            act(z_copy(2, slot))

    def project(step, share, head):
        base = share * 2 * width

        def chunk(at, total):
            take = pl.ds(pl.multiple_of(base + at * depth, LANE), depth)
            block = jnp.concatenate([paired[head, take, :], paired[head + 1, take, :]], axis=1)
            return total + dot(wide[:, lanes(at, depth)], block)

        first = jnp.zeros((2 * FLEN, 2 * HEAD), F32) if step == 0 else acc[head // 2]
        return lax.fori_loop(0, 2 * width // depth, chunk, first)

    for step in range(shares):
        share = (mine + step) % shares
        if step > 0:
            for piece in range(PLANE):
                gated_copy(step, share, piece).wait_recv()

        def widen(column, _):
            both = dot(gall[share, :, lanes(column)], spread).astype(BF16)
            wide[:FLEN, lanes(column, 2 * LANE)] = both[:, :2 * LANE]
            wide[FLEN:, lanes(column, 2 * LANE)] = both[:, 2 * LANE:]
            return 0

        lax.fori_loop(0, width // LANE, widen, 0)
        for head in range(0, heads, 2):
            weights_copy(share, head).wait()
            weights_copy(share, head + 1).wait()
            total = project(step, share, head)
            if step < shares - 1:
                acc[head // 2] = total
                continue
            for one in range(2):
                group, at = (head + one) // heads_part, (head + one) % heads_part
                cut = total[:, one * HEAD:(one + 1) * HEAD].astype(BF16)
                qsend[group, :, at * HEAD:(at + 1) * HEAD] = cut[:FLEN]
                ksend[group, :, at * HEAD:(at + 1) * HEAD] = cut[FLEN:]
                if at == heads_part - 1:
                    @pl.when(group != place)
                    def _():
                        k_copy(group, place).start()
                        q_copy(group, place).start()

                    @pl.when(group == place)
                    def _():
                        kbuf[rows(BACK + place), :] = ksend[group]
                        qbuf[place] = qsend[group]
                        pass_on(place, lambda c: c.start())

    lax.fori_loop(0, 3 * PLANE, mark, 0)
    for column in range(part // LANE):
        shared(column)
        if column == 0:
            for step in range(1, PLANE):
                slot = (place + step) % PLANE
                k_copy(slot, slot).wait_recv()
                pass_on(slot, lambda c: c.start())
    for step in range(1, PLANE):
        slot = (place + step) % PLANE
        q_copy(slot, slot).wait_recv()
    for dist in (1, 2):
        @pl.when(plane >= dist)
        def _():
            for slot in range(dist - 1, PLANE):
                z_copy(dist, slot).wait_recv()

    def o_copy(group, slot):
        return remote(osend.at[group], obuf.at[slot], os_.at[group], or_.at[slot], ctx=plane * PLANE + group)

    key_at = lax.broadcasted_iota(jnp.int32, (FLEN, SPAN * FLEN), 1)
    query_at = lax.broadcasted_iota(jnp.int32, (FLEN, SPAN * FLEN), 0)
    for block in range(PLANE):
        least = (BACK - block - plane * PLANE) * FLEN
        allowed = (key_at <= query_at + BACK * FLEN) & (key_at >= least)

        def one_head(head, _):
            keys = kbuf[block * FLEN:(block + SPAN) * FLEN, lanes(head)]
            seen = values[block * FLEN:(block + SPAN) * FLEN, lanes(head)]
            scores = lax.dot_general(
                qbuf[block, :, lanes(head)], keys, (((1,), (1,)), ((), ())), preferred_element_type=F32
            ) * HEAD ** (-0.5)
            scores = jnp.where(allowed, scores, -1e30)
            weights = jnp.exp(scores - jnp.max(scores, axis=1, keepdims=True))
            row_sum = jnp.sum(weights, axis=1, keepdims=True)
            osend[block, :, lanes(head)] = (dot(weights.astype(BF16), seen) / row_sum).astype(BF16)
            return 0

        lax.fori_loop(0, heads_part, one_head, 0)

        @pl.when(block != place)
        def _():
            o_copy(block, place).start()

        @pl.when(block == place)
        def _():
            obuf[place] = osend[block]

    for step in range(1, PLANE):
        slot = (place + step) % PLANE
        o_copy(slot, slot).wait_recv()
    for slot in range(PLANE):
        out_ref[:, slot * part:(slot + 1) * part] = obuf[slot]
    for step in range(1, shares):
        for piece in range(PLANE):
            gated_copy(step, mine, piece).wait_send()
    partners(1, lambda *a: ids_copy(*a).wait_send())
    for step in range(1, PLANE):
        slot = (place + step) % PLANE
        k_copy(slot, place).wait_send()
        q_copy(slot, place).wait_send()
        o_copy(slot, place).wait_send()
    for slot in range(PLANE):
        pass_on(slot, lambda c: c.wait_send())


def shards(token_ids, stream_table, filters, proj_qk):
    count, shares = lax.axis_size("ctx"), lax.axis_size("tp")
    width, vocab = stream_table.shape[2], stream_table.shape[1]
    heads, part = width // HEAD, width // PLANE
    channels = proj_qk.shape[0]
    by_head = proj_qk.reshape(channels, 2, heads, HEAD).transpose(0, 2, 1, 3)
    vmem, hbm = pl.BlockSpec(memory_space=pltpu.VMEM), pl.BlockSpec(memory_space=pl.ANY)
    dma = pltpu.SemaphoreType.DMA
    return pl.pallas_call(
        functools.partial(whole_kernel, count, shares),
        out_shape=jax.ShapeDtypeStruct((FLEN, width), BF16),
        in_specs=[vmem, vmem, hbm, hbm],
        out_specs=vmem,
        scratch_shapes=[
            pltpu.VMEM((3 * PLANE, 1, FLEN), jnp.int32),
            pltpu.VMEM((3, vocab, width), BF16),
            pltpu.VMEM((3 * PLANE * FLEN, vocab), BF16),
            pltpu.VMEM((LANE // GROUP * FLEN, 2 * FLEN), BF16),
            pltpu.VMEM((3 * PLANE * FLEN, LANE), BF16),
            pltpu.VMEM((3 * PLANE * FLEN, LANE), F32),
            pltpu.VMEM((SLOTS * FLEN, part), BF16),
            pltpu.VMEM((shares, FLEN, width), BF16),
            pltpu.VMEM((2 * FLEN, 2 * width), BF16),
            pltpu.VMEM((heads, channels, 2, HEAD), BF16),
            pltpu.VMEM((heads // 2, 2 * FLEN, 2 * HEAD), F32),
            pltpu.VMEM((PLANE, FLEN, part), BF16),
            pltpu.VMEM((PLANE, FLEN, part), BF16),
            pltpu.VMEM((PLANE, FLEN, part), BF16),
            pltpu.VMEM((SLOTS * FLEN, part), BF16),
            pltpu.VMEM((PLANE, FLEN, part), BF16),
            pltpu.VMEM((PLANE, FLEN, part), BF16),
            dma((3,)), dma((3 * PLANE,)), dma((3 * PLANE,)),
            dma((shares, PLANE)), dma((shares, PLANE)), dma((shares, heads)),
            dma((PLANE,)), dma((PLANE,)), dma((PLANE,)), dma((SLOTS,)),
            dma((2, PLANE)), dma((PLANE,)), dma((PLANE,)),
        ],
        compiler_params=pltpu.CompilerParams(
            collective_id=0, has_side_effects=True, vmem_limit_bytes=60 << 20
        ),
        name="hyena_attention",
    )(token_ids.reshape(1, FLEN), filters, stream_table, by_head)


def solution(mesh):
    placed = (P("ctx"), P(None, None, "tp"), P("tp", None), P(None, None, "tp"))
    return jax.shard_map(
        shards, mesh=mesh, in_specs=placed, out_specs=P("ctx", "tp"), check_vma=False
    )
```

```python
import functools
import jax
import jax.numpy as jnp
from jax import lax
from jax.experimental import pallas as pl
from jax.experimental.pallas import tpu as pltpu
from jax.sharding import PartitionSpec as P

HEAD = 128
GROUP = 16
FLEN = 128
SPAN = 8
LANE = 128
PLANE = 4
BACK = SPAN - 1
SLOTS = BACK + PLANE
MESH = pl.DeviceIdType.MESH
F32, BF16 = jnp.float32, jnp.bfloat16


def lanes(index, width=LANE):
    return pl.ds(pl.multiple_of(index * width, LANE), width)


def rows(index, count=1):
    return pl.ds(pl.multiple_of(index * FLEN, FLEN), count * FLEN)


def dot(a, b):
    return jnp.dot(a, b, preferred_element_type=F32)


def wait_ahead(barrier, ahead, always, each):
    for planes in range(3):
        @pl.when(ahead == planes if planes < 2 else ahead >= planes)
        def _():
            pl.semaphore_wait(barrier, always + planes * each)


def whole_kernel(
    count, shares, ids_ref, taps_ref, table_ref, weight_ref, out_ref,
    idbuf, table, onehot, toep, mixed, post, values,
    gall, wide, held, acc, qsend, ksend, qbuf, kbuf, osend, obuf,
    ts, isend, irecv, gs, gr, ws, qs, qr, ks, kr, zs, os_, or_,
):
    width = out_ref.shape[1]
    heads = width // HEAD
    part = width // PLANE
    heads_part = heads // PLANE
    vocab = table.shape[1]
    me, mine = lax.axis_index("ctx"), lax.axis_index("tp")
    plane, place = me // PLANE, me % PLANE
    planes = count // PLANE

    def table_copy(stream):
        return pltpu.make_async_copy(table_ref.at[stream], table.at[stream], ts.at[stream])

    def weights_copy(share, piece):
        cut = pl.ds(share * width + piece * part, part)
        return pltpu.make_async_copy(weight_ref.at[cut], held.at[cut], ws.at[share, piece])

    for stream in range(3):
        table_copy(stream).start()
    for step in range(shares):
        for piece in range(PLANE):
            weights_copy((mine + step) % shares, piece).start()

    idbuf[...] = jnp.full(idbuf.shape, -1, jnp.int32)
    idbuf[2 * PLANE + place] = ids_ref[...]
    kbuf[:BACK * FLEN] = jnp.zeros((BACK * FLEN, part), BF16)
    barrier = pltpu.get_barrier_semaphore()

    def greet(**device):
        pl.semaphore_signal(barrier, inc=1, device_id=device, device_id_type=MESH)

    def partners(sign, act):
        for dist in range(3):
            for other in range(PLANE):
                there = plane + sign * dist
                ok = (there >= 0) & (there < planes)
                if dist == 0:
                    ok = ok & (other != place)
                pl.when(ok)(functools.partial(act, dist, other, there * PLANE + other))

    for step in range(1, shares):
        greet(tp=(mine + step) % shares)
    partners(-1, lambda dist, other, device: greet(ctx=device))
    ahead = planes - 1 - plane
    for some in range(3):
        @pl.when(ahead == some if some < 2 else ahead >= some)
        def _():
            pl.semaphore_wait(barrier, shares - 1 + PLANE - 1 + some * PLANE)

    def remote(src, dst, send, recv, **device):
        return pltpu.make_async_remote_copy(
            src_ref=src, dst_ref=dst, send_sem=send, recv_sem=recv, device_id=device, device_id_type=MESH
        )

    def ids_copy(dist, other, device):
        slot = 2 * PLANE + place - dist * PLANE
        return remote(ids_ref, idbuf.at[slot], isend.at[dist * PLANE + other], irecv.at[slot], ctx=device)

    def ids_here(dist, other, device):
        slot = 2 * PLANE + other - dist * PLANE
        remote(ids_ref, idbuf.at[slot], isend.at[0], irecv.at[slot], ctx=device).wait_recv()

    partners(1, lambda *a: ids_copy(*a).start())
    partners(-1, ids_here)

    def mark(block, _):
        ids = jnp.transpose(jnp.broadcast_to(idbuf[block].astype(F32), (FLEN, FLEN)))
        word = lax.broadcasted_iota(jnp.int32, (FLEN, LANE), 1).astype(F32)
        for at in range(vocab // LANE):
            onehot[rows(block), at * LANE:(at + 1) * LANE] = (ids == word + float(at * LANE)).astype(F32).astype(BF16)
        return 0

    lax.fori_loop(BACK + place, BACK + place + 2, mark, 0)
    row = lax.broadcasted_iota(jnp.int32, (FLEN, FLEN), 0)
    col = lax.broadcasted_iota(jnp.int32, (FLEN, FLEN), 1)
    flip = ((row + col == FLEN) | (row + col == 0)).astype(F32).astype(BF16)
    after = (row >= col).astype(F32).astype(BF16)
    before = (row < col).astype(F32).astype(BF16)
    per = LANE // GROUP

    def build(column):
        line = dot(taps_ref[pl.ds(pl.multiple_of(column * per, per), per), :].astype(BF16), flip)
        for g in range(per):
            turned = pltpu.roll(
                jnp.broadcast_to(line[g:g + 1], (FLEN, FLEN)), 0, 1, stride=1, stride_axis=0
            ).astype(BF16)
            toep[g * FLEN:(g + 1) * FLEN, :FLEN] = turned * before
            toep[g * FLEN:(g + 1) * FLEN, FLEN:] = turned * after

    def convolve(window):
        group_of = lax.broadcasted_iota(jnp.int32, (FLEN, window.shape[1]), 1) % LANE // GROUP
        every = dot(toep[...], window)
        total = every[:FLEN]
        for g in range(1, per):
            total = jnp.where(group_of == g, every[g * FLEN:(g + 1) * FLEN], total)
        return total

    def pair_of(cols):
        return jnp.concatenate([table[1, :, cols], table[2, :, cols]], axis=1)

    def own(column, _):
        cols = lanes(column)
        both = dot(onehot[rows(BACK + place, 2), :], pair_of(cols))
        window = (both[:, :LANE] * both[:, LANE:]).astype(BF16)
        gate = dot(onehot[rows(BACK + 1 + place), :], table[0, :, cols])
        build(column)
        gall[mine, :, cols] = (gate * convolve(window)).astype(BF16)
        return 0

    def gated_copy(step, slot, piece):
        cut = gall.at[slot, :, piece * part:(piece + 1) * part]
        return remote(cut, cut, gs.at[step, piece], gr.at[slot, piece], tp=(mine + step) % shares)

    for stream in range(3):
        table_copy(stream).wait()
    for piece in range(PLANE):
        lax.fori_loop(piece * (part // LANE), (piece + 1) * (part // LANE), own, 0)
        for step in range(1, shares):
            gated_copy(step, mine, piece).start()

    def shared(step):
        column = place * (part // LANE) + step
        cols = lanes(column)
        build(column)

        def fill(some, _):
            marks = onehot[pl.ds(pl.multiple_of(some * PLANE * FLEN, FLEN), PLANE * FLEN), :]
            here = pl.ds(pl.multiple_of(some * PLANE * FLEN, FLEN), PLANE * FLEN)
            both = dot(marks, pair_of(cols))
            mixed[here, :] = (both[:, :LANE] * both[:, LANE:]).astype(BF16)
            post[here, :] = dot(marks, table[0, :, cols])
            return 0

        lax.fori_loop(0, 3, fill, 0)

        def two_windows(twice, _):
            block = 2 * twice
            conv = convolve(jnp.concatenate([mixed[rows(block, 2), :], mixed[rows(block + 1, 2), :]], axis=1))
            values[rows(block), step * LANE:(step + 1) * LANE] = (post[rows(block + 1), :] * conv[:, :LANE]).astype(BF16)
            values[rows(block + 1), step * LANE:(step + 1) * LANE] = (post[rows(block + 2), :] * conv[:, LANE:]).astype(BF16)
            return 0

        lax.fori_loop(0, SLOTS // 2, two_windows, 0)
        conv = convolve(mixed[(SLOTS - 1) * FLEN:(SLOTS + 1) * FLEN, :])
        values[(SLOTS - 1) * FLEN:, step * LANE:(step + 1) * LANE] = (post[SLOTS * FLEN:, :] * conv).astype(BF16)

    src = lax.broadcasted_iota(jnp.int32, (LANE, 4 * LANE), 0)
    dst = lax.broadcasted_iota(jnp.int32, (LANE, 4 * LANE), 1)
    spread = (dst == jnp.where(dst < 2 * LANE, 2 * src, 2 * src + 1 + 2 * LANE)).astype(F32).astype(BF16)
    depth = min(2 * width, 1024)

    def q_copy(group, slot):
        return remote(qsend.at[group], qbuf.at[slot], qs.at[group], qr.at[slot], ctx=plane * PLANE + group)

    def k_copy(group, slot):
        return remote(ksend.at[group], kbuf.at[rows(BACK + slot)], ks.at[group], kr.at[BACK + slot], ctx=plane * PLANE + group)

    def z_copy(dist, slot):
        to = BACK + slot - dist * PLANE
        return remote(kbuf.at[rows(BACK + slot)], kbuf.at[rows(to)], zs.at[dist - 1, slot], kr.at[to], ctx=me + dist * PLANE)

    def pass_on(slot, act):
        @pl.when(plane + 1 < planes)
        def _():
            act(z_copy(1, slot))

        @pl.when((plane + 2 < planes) & (slot >= 1))
        def _():
            act(z_copy(2, slot))

    def project(step, share, head):
        def chunk(at, total):
            take = pl.ds(share * width + at * (depth // 2), depth // 2)
            block = jnp.concatenate(
                [held[take, head].reshape(depth, HEAD), held[take, head + 1].reshape(depth, HEAD)], axis=1
            )
            return total + dot(wide[:, lanes(at, depth)], block)

        first = jnp.zeros((2 * FLEN, 2 * HEAD), F32) if step == 0 else acc[head // 2]
        return lax.fori_loop(0, 2 * width // depth, chunk, first)

    for step in range(shares):
        share = (mine + step) % shares
        if step > 0:
            for piece in range(PLANE):
                gated_copy(step, share, piece).wait_recv()

        def widen(column, _):
            both = dot(gall[share, :, lanes(column)], spread).astype(BF16)
            wide[:FLEN, lanes(column, 2 * LANE)] = both[:, :2 * LANE]
            wide[FLEN:, lanes(column, 2 * LANE)] = both[:, 2 * LANE:]
            return 0

        lax.fori_loop(0, width // LANE, widen, 0)
        for piece in range(PLANE):
            weights_copy(share, piece).wait()
        for head in range(0, heads, 2):
            total = project(step, share, head)
            if step < shares - 1:
                acc[head // 2] = total
                continue
            for one in range(2):
                group, at = (head + one) // heads_part, (head + one) % heads_part
                cut = total[:, one * HEAD:(one + 1) * HEAD].astype(BF16)
                qsend[group, :, at * HEAD:(at + 1) * HEAD] = cut[:FLEN]
                ksend[group, :, at * HEAD:(at + 1) * HEAD] = cut[FLEN:]
                if at == heads_part - 1:
                    @pl.when(group != place)
                    def _():
                        k_copy(group, place).start()
                        q_copy(group, place).start()

                    @pl.when(group == place)
                    def _():
                        kbuf[rows(BACK + place), :] = ksend[group]
                        qbuf[place] = qsend[group]
                        pass_on(place, lambda c: c.start())

    lax.fori_loop(0, 3 * PLANE, mark, 0)
    for column in range(part // LANE):
        shared(column)
        if column == 0:
            for step in range(1, PLANE):
                slot = (place + step) % PLANE
                k_copy(slot, slot).wait_recv()
                pass_on(slot, lambda c: c.start())
    for step in range(1, PLANE):
        slot = (place + step) % PLANE
        q_copy(slot, slot).wait_recv()
    for dist in (1, 2):
        @pl.when(plane >= dist)
        def _():
            for slot in range(dist - 1, PLANE):
                z_copy(dist, slot).wait_recv()

    def o_copy(group, slot):
        return remote(osend.at[group], obuf.at[slot], os_.at[group], or_.at[slot], ctx=plane * PLANE + group)

    key_at = lax.broadcasted_iota(jnp.int32, (FLEN, SPAN * FLEN), 1)
    query_at = lax.broadcasted_iota(jnp.int32, (FLEN, SPAN * FLEN), 0)
    for block in range(PLANE):
        least = (BACK - block - plane * PLANE) * FLEN
        allowed = (key_at <= query_at + BACK * FLEN) & (key_at >= least)

        def one_head(head, _):
            keys = kbuf[block * FLEN:(block + SPAN) * FLEN, lanes(head)]
            seen = values[block * FLEN:(block + SPAN) * FLEN, lanes(head)]
            scores = lax.dot_general(
                qbuf[block, :, lanes(head)], keys, (((1,), (1,)), ((), ())), preferred_element_type=F32
            ) * HEAD ** (-0.5)
            scores = jnp.where(allowed, scores, -1e30)
            weights = jnp.exp(scores - jnp.max(scores, axis=1, keepdims=True))
            row_sum = jnp.sum(weights, axis=1, keepdims=True)
            osend[block, :, lanes(head)] = (dot(weights.astype(BF16), seen) / row_sum).astype(BF16)
            return 0

        lax.fori_loop(0, heads_part, one_head, 0)

        @pl.when(block != place)
        def _():
            o_copy(block, place).start()

        @pl.when(block == place)
        def _():
            obuf[place] = osend[block]

    for step in range(1, PLANE):
        slot = (place + step) % PLANE
        o_copy(slot, slot).wait_recv()
    for slot in range(PLANE):
        out_ref[:, slot * part:(slot + 1) * part] = obuf[slot]
    for step in range(1, shares):
        for piece in range(PLANE):
            gated_copy(step, mine, piece).wait_send()
    partners(1, lambda *a: ids_copy(*a).wait_send())
    for step in range(1, PLANE):
        slot = (place + step) % PLANE
        k_copy(slot, place).wait_send()
        q_copy(slot, place).wait_send()
        o_copy(slot, place).wait_send()
    for slot in range(PLANE):
        pass_on(slot, lambda c: c.wait_send())


def shards(token_ids, stream_table, filters, proj_qk):
    count, shares = lax.axis_size("ctx"), lax.axis_size("tp")
    width, vocab = stream_table.shape[2], stream_table.shape[1]
    heads, part = width // HEAD, width // PLANE
    channels = proj_qk.shape[0]
    by_head = proj_qk.reshape(channels, 2, heads, HEAD).transpose(0, 2, 1, 3)
    vmem, hbm = pl.BlockSpec(memory_space=pltpu.VMEM), pl.BlockSpec(memory_space=pl.ANY)
    dma = pltpu.SemaphoreType.DMA
    return pl.pallas_call(
        functools.partial(whole_kernel, count, shares),
        out_shape=jax.ShapeDtypeStruct((FLEN, width), BF16),
        in_specs=[vmem, vmem, hbm, hbm],
        out_specs=vmem,
        scratch_shapes=[
            pltpu.VMEM((3 * PLANE, 1, FLEN), jnp.int32),
            pltpu.VMEM((3, vocab, width), BF16),
            pltpu.VMEM((3 * PLANE * FLEN, vocab), BF16),
            pltpu.VMEM((LANE // GROUP * FLEN, 2 * FLEN), BF16),
            pltpu.VMEM((3 * PLANE * FLEN, LANE), BF16),
            pltpu.VMEM((3 * PLANE * FLEN, LANE), F32),
            pltpu.VMEM((SLOTS * FLEN, part), BF16),
            pltpu.VMEM((shares, FLEN, width), BF16),
            pltpu.VMEM((2 * FLEN, 2 * width), BF16),
            pltpu.VMEM((channels, heads, 2, HEAD), BF16),
            pltpu.VMEM((heads // 2, 2 * FLEN, 2 * HEAD), F32),
            pltpu.VMEM((PLANE, FLEN, part), BF16),
            pltpu.VMEM((PLANE, FLEN, part), BF16),
            pltpu.VMEM((PLANE, FLEN, part), BF16),
            pltpu.VMEM((SLOTS * FLEN, part), BF16),
            pltpu.VMEM((PLANE, FLEN, part), BF16),
            pltpu.VMEM((PLANE, FLEN, part), BF16),
            dma((3,)), dma((3 * PLANE,)), dma((3 * PLANE,)),
            dma((shares, PLANE)), dma((shares, PLANE)), dma((shares, PLANE)),
            dma((PLANE,)), dma((PLANE,)), dma((PLANE,)), dma((SLOTS,)),
            dma((2, PLANE)), dma((PLANE,)), dma((PLANE,)),
        ],
        compiler_params=pltpu.CompilerParams(
            collective_id=0, has_side_effects=True, vmem_limit_bytes=60 << 20
        ),
        name="hyena_attention",
    )(token_ids.reshape(1, FLEN), filters, stream_table, by_head)


def solution(mesh):
    placed = (P("ctx"), P(None, None, "tp"), P("tp", None), P(None, None, "tp"))
    return jax.shard_map(
        shards, mesh=mesh, in_specs=placed, out_specs=P("ctx", "tp"), check_vma=False
    )
```
